256 devices in a mesh: region: 64 (over x, z, core), mode: 4 (over y).
Axes of the slice: x: 4, y: 4, z: 8, core: 2. Of those that a mesh axis runs over, the one named last changes fastest.
Arguments:
- modes: bfloat16 [6, 64, 262144], P(None, 'mode', 'region'), may hold values from -1.1953125 to 1.1953125
- stiffness: bfloat16 [6, 4, 6, 4, 262144], P(None, None, None, None, 'region'), may hold values from -1.25 to 1.25
- mass_ref: bfloat16 [6, 4, 6, 4], replicated, may hold values from -1.25 to 1.25
- areas: float32 [262144], P('region'), may hold values from 0.5 to 2
- eigenvalues: float32 [64], P('mode'), may hold values from 0.5 to 4
- send_list: int32 [4, 8192], P(None, 'region'), may hold values from 0 to 4095, as said below
- connect: int32 [4, 262144], P(None, 'region'), may hold values from 0 to 4607, as said below
- block_var: int32 [8192], P('region'), may hold values from 0 to 8191, as said below
- mode_weight: float32 [64], P('mode'), may hold values from 0.25 to 4
Outputs:
- sens: float32 [64, 8192], P('mode', 'region')
- aggregate: float32 [8192], P('region')
The draws below stay inside these ranges and needn't reach their ends.
Inputs may be any that keep to these rules, and one draw needn't show every extreme that they name: `send_list`: each region's list for one direction names 128 distinct local nodes. `connect`: A number below 4096 is an owned node; 4096 + d * 128 + s is entry s of direction d in the extended list, used only where region r - o_d exists. `block_var`: A block of region r names a variable v with v // 128 in r - 1, r, r + 1.
All inputs are finite; a program needn't handle non-finite values.
Results may differ from the reference program's by a relative error of at most 0.0003.
Values may be sent and summed in bfloat16 or wider, within the bound.
No kernel may reach another device: no remote copies, remote signals or barrier semaphores. Data moves between devices by JAX's collectives and lax.ppermute only.
A program may use at most 192 MiB of HBM per device.

```python
import math
import jax
import jax.numpy as jnp
from jax import lax

MODES = 64
NODE_DEV = 4096
ELEM_DEV = 4096
SLOTS = 128
BLOCK = 32
VAR_DEV = 128
NODES = 262144
ELEMENTS = 262144
VARS = 8192
N_REGION = 64


def draw_send_list(key, part):
    key = jax.random.fold_in(key, 11)
    regions = ELEMENTS // ELEM_DEV
    keys = jax.random.split(key, 4 * regions)
    picks = jax.vmap(lambda one_key: jax.random.permutation(one_key, NODE_DEV)[:SLOTS])(keys)
    return picks.reshape(4, regions * SLOTS).astype(jnp.int32)


def draw_connect(key, part):
    key = jax.random.fold_in(key, 12)
    regions = ELEMENTS // ELEM_DEV
    corners = jax.random.randint(key, (4, ELEMENTS), 0, NODE_DEV, dtype=jnp.int32)
    index = jnp.arange(ELEMENTS, dtype=jnp.int32)
    local = index % ELEM_DEV
    region_of = index // ELEM_DEV
    stride = ELEM_DEV // (4 * SLOTS)
    ghost = local // stride
    direction = jnp.clip(ghost // SLOTS, 0, 3)
    offsets = jnp.array([1, -1, 2, -2], dtype=jnp.int32)
    source = region_of - offsets[direction]
    used = (local % stride == 0) & (ghost < 4 * SLOTS) & (source >= 0) & (source < regions)
    first = jnp.where(used, NODE_DEV + ghost, corners[0])
    return corners.at[0].set(first.astype(jnp.int32))


def draw_block_var(key, part):
    key = jax.random.fold_in(key, 13)
    regions = ELEMENTS // ELEM_DEV
    blocks_all = ELEMENTS // BLOCK
    per_region = ELEM_DEV // BLOCK
    first_key, second_key = jax.random.split(key)
    region_of = jnp.arange(blocks_all, dtype=jnp.int32) // per_region
    owner = jnp.clip(region_of + jax.random.randint(first_key, (blocks_all,), -1, 2, dtype=jnp.int32), 0, regions - 1)
    chosen = owner * VAR_DEV + jax.random.randint(second_key, (blocks_all,), 0, VAR_DEV, dtype=jnp.int32)
    chosen = chosen.at[0].set(0).at[blocks_all - 1].set(VARS - 1)
    return chosen.astype(jnp.int32)


def block_levels(rng, dims, cuts, least, top_value):
    gain, own = 1.0, jax.random.fold_in(rng, 6)
    for dim, shards_of in cuts:
        steps = jnp.exp(jax.random.uniform(jax.random.fold_in(own, dim), (shards_of,), jnp.float32, least / len(cuts), top_value / len(cuts)))
        gain = gain * jnp.repeat(steps, dims[dim] // shards_of).reshape([-1 if axis == dim else 1 for axis in range(len(dims))])
    return gain


def centred(stream_key, dims, deviation, bound, cuts=(), kind=jnp.bfloat16):
    level = block_levels(stream_key, dims, cuts, -0.22, 0.18) if cuts else 1.0
    result = jax.random.normal(stream_key, dims, jnp.float32) * deviation * level
    return jnp.minimum(jnp.maximum(result, -bound), bound).astype(kind)


def setup_inputs(seed: int = 0) -> dict:
    arg_keys = jax.random.split(jax.random.key(seed), 10)
    return {
        "modes": centred(arg_keys[0], (6, MODES, NODES), 0.2, 1.1953125, ((1, 4), (2, 64))),
        "stiffness": centred(arg_keys[1], (6, 4, 6, 4, ELEMENTS), 24 ** -0.5, 1.25, ((4, 64),)),
        "mass_ref": centred(arg_keys[2], (6, 4, 6, 4), 24 ** -0.5, 1.25),
        "areas": jnp.clip(jnp.exp(math.log(2.0) - 1.3862944 * jax.random.uniform(arg_keys[3], (ELEMENTS,), jnp.float32) ** block_levels(arg_keys[3], (ELEMENTS,), ((0, 64),), -0.2, 0.2)), 0.5, 2.0),
        "eigenvalues": jnp.clip(jnp.exp(math.log(4.0) - 2.0794415 * jax.random.uniform(arg_keys[4], (MODES,), jnp.float32) ** block_levels(arg_keys[4], (MODES,), ((0, 4),), -0.2, 0.2)), 0.5, 4.0),
        "send_list": draw_send_list(jax.random.fold_in(arg_keys[9], 71), 0),
        "connect": draw_connect(jax.random.fold_in(arg_keys[9], 71), 0),
        "block_var": draw_block_var(jax.random.fold_in(arg_keys[9], 71), 0),
        "mode_weight": jnp.clip(jnp.exp(math.log(4.0) - 2.7725887 * jax.random.uniform(arg_keys[8], (MODES,), jnp.float32) ** block_levels(arg_keys[8], (MODES,), ((0, 4),), -0.2, 0.2)), 0.25, 4.0),
    }


OFFSETS = (1, -1, 2, -2)


def reference(modes, stiffness, mass_ref, areas, eigenvalues, send_list, connect, block_var, mode_weight):
    region_ids = jnp.arange(N_REGION, dtype=jnp.int32)
    columns = [region_ids[:, None] * NODE_DEV + jnp.arange(NODE_DEV, dtype=jnp.int32)[None, :]]
    for direction, offset in enumerate(OFFSETS):
        source = region_ids - offset
        inside = (source >= 0) & (source < N_REGION)
        clipped = jnp.clip(source, 0, N_REGION - 1)
        lists = send_list[direction].reshape(N_REGION, SLOTS)[clipped]
        global_ids = jnp.where(inside[:, None], clipped[:, None] * NODE_DEV + lists, NODES)
        columns.append(global_ids.astype(jnp.int32))
    table = jnp.concatenate(columns, axis=1).astype(jnp.int32)
    padded = jnp.concatenate([modes, jnp.zeros((6, MODES, 1), modes.dtype)], axis=2)
    mass_full = mass_ref.astype(jnp.float32)

    def one_region(region):
        start = (region * ELEM_DEV).astype(jnp.int32)
        local = lax.dynamic_slice_in_dim(connect, start, ELEM_DEV, 1)
        global_ids = table[region][local]
        rows = padded[:, :, global_ids].astype(jnp.float32)
        kmat = lax.dynamic_slice_in_dim(stiffness, start, ELEM_DEV, 4).astype(jnp.float32)
        area = lax.dynamic_slice_in_dim(areas, start, ELEM_DEV, 0)
        stiff_rows = jnp.einsum("kmcl,kcjdl->jmdl", rows, kmat, precision=lax.Precision.HIGHEST)
        mass_rows = jnp.einsum("kmcl,kcjd->jmdl", rows, mass_full, precision=lax.Precision.HIGHEST)
        stiff_part = jnp.sum(stiff_rows * rows, axis=(0, 2))
        mass_part = jnp.sum(mass_rows * rows, axis=(0, 2))
        energy = stiff_part - eigenvalues[:, None] * area[None, :] * mass_part
        return jnp.sum(energy.reshape(MODES, ELEM_DEV // BLOCK, BLOCK), axis=2)

    block_sums = lax.map(one_region, region_ids)
    block_sums = jnp.transpose(block_sums, (0, 2, 1)).reshape(-1, MODES)
    sens = jax.ops.segment_sum(block_sums, block_var, num_segments=VARS).T
    aggregate = jnp.dot(mode_weight, sens, precision=lax.Precision.HIGHEST)
    return sens, aggregate
```

```python
import jax, jax.numpy as jnp
from jax import lax
from jax.experimental import pallas as pl
from jax.sharding import PartitionSpec as P
from jax.experimental.pallas import tpu as pltpu

NT = (((1,), (1,)), ((), ()))
SLOTS, VAR_DEV = 128, 128
f32, bf16 = jnp.float32, jnp.bfloat16


def split3(x):
    hi = x.astype(bf16)
    rest = x - hi.astype(f32)
    mid = rest.astype(bf16)
    low = (rest - mid.astype(f32)).astype(bf16)
    return jnp.concatenate([hi, mid, low], axis=0)


def fill_table(modes, table, tiles):
    def step(n, _):
        col = pl.ds(pl.multiple_of(n * 128, 128), 128)
        x = modes[:, col].astype(f32)
        x = jnp.concatenate([x, jnp.zeros((32, 128), f32)], axis=0)
        table[col, :] = x.T
        return 0
    lax.fori_loop(0, tiles, step, 0, unroll=2)


def send_kernel(modes, send_list, order, out0, out1, out2, out3, table):
    nodes = modes.shape[1]
    fill_table(modes, table, nodes // 128)
    for d, out in enumerate((out0, out1, out2, out3)):
        base = order[d] * SLOTS
        def step(s8, _):
            rows = [table[pl.ds(send_list[base + s8 * 16 + r], 1), :] for r in range(16)]
            out[pl.ds(pl.multiple_of(s8 * 16, 16), 16), :] = jnp.concatenate(rows, axis=0).astype(bf16)
            return 0
        lax.fori_loop(0, 8, step, 0)


PER = 8

def main_kernel(modes, ghost0, ghost1, ghost2, ghost3, order, stiff, weights, areas, lam, connect, var, own, near, far,
                table, gather_a, gather_b, f_buf, s_buf, u_buf, m_buf, *bufs):
    kbufs, ibufs, ksem, isem = bufs[:4], bufs[4:12], bufs[12], bufs[13]
    nodes = modes.shape[1]
    tiles = connect.shape[1] // 128
    gathers = (gather_a, gather_b)

    def k_copy(t, slot):
        return pltpu.make_async_copy(
            stiff.at[:, :, :, :, pl.ds(pl.multiple_of(t * 128, 128), 128)], kbufs[slot], ksem.at[slot])

    def i_copy(t, slot):
        return pltpu.make_async_copy(
            connect.at[:, pl.ds(pl.multiple_of(t * 128, 128), 128)], ibufs[slot], isem.at[slot])

    i_copy(0, PER - 1).start()
    for q in range(PER - 1):
        i_copy(q + 1, q).start()
    for q in range(4):
        k_copy(q, q).start()
    fill_table(modes, table, nodes // 128)
    for d, ghost in enumerate((ghost0, ghost1, ghost2, ghost3)):
        place = (order[d ^ 1]) * SLOTS
        table[pl.ds(pl.multiple_of(nodes + place, 128), SLOTS), :] = ghost[...].astype(f32)
    lane = lax.broadcasted_iota(jnp.int32, (128, 128), 1)
    row = lax.broadcasted_iota(jnp.int32, (128, 128), 0)
    eye = (lane == row).astype(bf16)[:96]
    summing = (row // 32 == lane).astype(bf16)

    def gather_rows(slot, dest):
        for e8 in range(0, 128, 8):
            for c in range(4):
                rows = [table[pl.ds(ibufs[slot][c, e8 + r], 1), :] for r in range(8)]
                dest[c, e8:e8 + 8, :] = jnp.concatenate(rows, axis=0)

    i_copy(0, PER - 1).wait()
    gather_rows(PER - 1, gather_a)
    i_copy(PER, PER - 1).start()

    def compute(t, kbuf, rows):
        for a in range(6):
            for c in range(4):
                for b in range(6):
                    first = ((a * 4 + c) * 6 + b) * 4
                    f_buf[first:first + 4, :] = kbuf[a, c, b].astype(f32)
        for i in range(24):
            for jb in range(i // 8, 3):
                s_buf[i * 24 + jb * 8:i * 24 + jb * 8 + 8, :] = (
                    f_buf[i * 24 + jb * 8:i * 24 + jb * 8 + 8, :] + f_buf[pl.ds(jb * 8 * 24 + i, 8, stride=24), :])
        g = [rows[c].astype(bf16) for c in range(4)]
        for c in range(4):
            u_buf[c] = lax.dot_general(eye, g[c], NT, preferred_element_type=f32)
        m_buf[...] = lax.dot_general(weights[...], jnp.concatenate(g, axis=1), NT, preferred_element_type=f32)
        out = []
        for h in range(2):
            u = [u_buf[c, k * 16 + h * 8:k * 16 + h * 8 + 8, :] for k in range(6) for c in range(4)]
            stiff_part = mass_part = None
            for i in range(24):
                acc = f_buf[i * 25:i * 25 + 1, :] * u[i]
                for j in range(i + 1, 24):
                    acc = acc + s_buf[i * 24 + j:i * 24 + j + 1, :] * u[j]
                stiff_part = acc * u[i] if stiff_part is None else stiff_part + acc * u[i]
                term = m_buf[i * 16 + h * 8:i * 16 + h * 8 + 8, :] * u[i]
                mass_part = term if mass_part is None else mass_part + term
            area = areas[pl.ds(t, 1), :]
            out.append(stiff_part - lam[h * 8:h * 8 + 8, :] * area * mass_part)
        energy = jnp.concatenate(out, axis=0)
        sums = jnp.dot(split3(energy), summing, preferred_element_type=f32)
        sums = sums[0:16] + sums[16:32] + sums[32:48]
        return pltpu.roll(sums, t * 4, 1)

    def body(it, blocks):
        for q in range(PER):
            t = it * PER + q
            i_copy(0, q).wait()
            k_copy(0, q % 4).wait()
            gather_rows(q, gathers[(q + 1) % 2])
            i_copy(jnp.minimum(t + PER + 1, tiles - 1), q).start()
            blocks = blocks + compute(t, kbufs[q % 4], gathers[q % 2])
            k_copy(jnp.minimum(t + 4, tiles - 1), q % 4).start()
        return blocks

    blocks = lax.fori_loop(0, tiles // PER, body, jnp.zeros((16, 128), f32))
    for q in range(PER):
        i_copy(0, q).wait()
    for q in range(4):
        k_copy(0, q).wait()
    table_t = (lax.broadcasted_iota(jnp.int32, (3 * VAR_DEV, 128), 0) == var[...]).astype(bf16)
    window = lax.dot_general(split3(blocks), table_t, NT, preferred_element_type=f32)
    window = window[0:16] + window[16:32] + window[32:48]
    for part, out in enumerate((own, near, far)):
        out[...] = window[:, part * VAR_DEV:(part + 1) * VAR_DEV]


VM = pl.BlockSpec(memory_space=pltpu.VMEM)
SM = pl.BlockSpec(memory_space=pltpu.SMEM)
HB = pl.BlockSpec(memory_space=pl.ANY)


def send_rows(modes, send_list, order):
    return pl.pallas_call(
        send_kernel,
        out_shape=[jax.ShapeDtypeStruct((SLOTS, 128), bf16)] * 4,
        in_specs=[VM, SM, SM], out_specs=(VM,) * 4,
        scratch_shapes=[pltpu.VMEM((modes.shape[1], 128), f32)],
        compiler_params=pltpu.CompilerParams(vmem_limit_bytes=16 * 2**20),
    )(modes, send_list, order)


def main_call(modes, ghosts, order, stiff, weights, areas, lam, connect, var):
    return pl.pallas_call(
        main_kernel,
        out_shape=[jax.ShapeDtypeStruct((16, VAR_DEV), f32)] * 3,
        in_specs=[VM, VM, VM, VM, VM, SM, HB, VM, VM, VM, HB, VM], out_specs=(VM,) * 3,
        scratch_shapes=[
            pltpu.VMEM((modes.shape[1] + 4 * SLOTS, 128), f32),
            pltpu.VMEM((4, 128, 128), f32), pltpu.VMEM((4, 128, 128), f32),
            pltpu.VMEM((576, 128), f32), pltpu.VMEM((576, 128), f32),
            pltpu.VMEM((4, 96, 128), f32), pltpu.VMEM((384, 128), f32),
            *[pltpu.VMEM((6, 4, 6, 4, 128), bf16)] * 4,
            *[pltpu.SMEM((4, 128), jnp.int32)] * PER,
            pltpu.SemaphoreType.DMA((4,)), pltpu.SemaphoreType.DMA((PER,)),
        ],
        compiler_params=pltpu.CompilerParams(vmem_limit_bytes=24 * 2**20),
    )(modes, *ghosts, order, stiff, weights, areas, lam, connect, var)


def mass_weights(mass_ref):
    m = mass_ref.reshape(24, 6, 4)
    eye = jnp.eye(16, dtype=mass_ref.dtype)
    w = jnp.einsum("ikc,mn->imckn", m, eye).reshape(384, 4, 96)
    return jnp.pad(w, ((0, 0), (0, 0), (0, 32))).reshape(384, 512)


OFFSETS = (1, -1, 2, -2)


def swap(array, axis, first):
    length = lax.axis_size(axis)
    pairs = []
    for i in range(first, length - 1, 2):
        pairs += [(i, i + 1), (i + 1, i)]
    return lax.ppermute(array, axis, pairs)


def swap_two(array, axis, first):
    length = lax.axis_size(axis)
    pairs = []
    for k in range(2 * first, length - 3, 4):
        for p in range(2):
            pairs += [(k + p, k + p + 2), (k + p + 2, k + p)]
    return lax.ppermute(array, axis, pairs)


def shards(
    modes, stiffness, mass_ref, areas, eigenvalues, send_list, connect, block_var, mode_weight
):
    region = lax.axis_index("region")
    mode_dev, node_count = modes.shape[1:]
    elem_count = connect.shape[1]
    flat = modes.reshape(6 * mode_dev, node_count)
    odd = region % 2
    upper = (region // 2) % 2
    order = jnp.stack([odd, 1 - odd, 2 + upper, 3 - upper]).astype(jnp.int32)
    sent = send_rows(flat, send_list.reshape(-1), order)
    received = [swap(sent[0], "region", 0), swap(sent[1], "region", 1),
                swap_two(sent[2], "region", 0), swap_two(sent[3], "region", 1)]
    step = block_var // VAR_DEV - region
    near = jnp.where(odd == 1, -1, 1)
    column = block_var % VAR_DEV + VAR_DEV * jnp.where(step == 0, 0, jnp.where(step == near, 1, 2))
    lam = jnp.broadcast_to(eigenvalues[:, None], (mode_dev, 128))
    own, sent_a, sent_b = main_call(
        flat, received, order, stiffness, mass_weights(mass_ref), areas.reshape(elem_count // 128, 128),
        lam, connect, column.reshape(1, 128))
    sens = own + swap(sent_a, "region", 0) + swap(sent_b, "region", 1)
    weighted = jnp.sum(mode_weight[:, None] * sens, axis=0)
    weighted = weighted + lax.ppermute(weighted, "mode", [(0, 1), (1, 0), (2, 3), (3, 2)])
    weighted = weighted + lax.ppermute(weighted, "mode", [(0, 3), (3, 0), (1, 2), (2, 1)])
    return (sens, weighted)


def solution(mesh):
    in_specs = (
        P(None, "mode", "region"),
        P(None, None, None, None, "region"),
        P(),
        P("region"),
        P("mode"),
        P(None, "region"),
        P(None, "region"),
        P("region"),
        P("mode"),
    )
    out_specs = (P("mode", "region"), P("region"))
    return jax.shard_map(shards, mesh=mesh, in_specs=in_specs, out_specs=out_specs, check_vma=False)
```

```python
import jax
import jax.numpy as jnp
from jax import lax
from jax.experimental import pallas as pl
from jax.experimental.pallas import tpu as pltpu
from jax.sharding import PartitionSpec as P

NT = (((1,), (1,)), ((), ()))
SLOTS, VAR_DEV = 128, 128
TILE, CHUNK = 128, 512
TILES = CHUNK // TILE
BESIDE = 0
f32, bf16 = jnp.float32, jnp.bfloat16


def iota(shape, dim):
    return lax.broadcasted_iota(jnp.int32, shape, dim)


def pieces(x):
    hi = x.astype(bf16)
    rest = x - hi.astype(f32)
    mid = rest.astype(bf16)
    low = (rest - mid.astype(f32)).astype(bf16)
    return jnp.concatenate([hi, mid, low], axis=0)


def mass_matrix(mass, stage, weights):
    stage[...] = jnp.zeros_like(stage)
    for a in range(6):
        for c in range(4):
            first = (a * 4 + c) * 4
            stage[first:first + 4, 0:6] = mass[a, c].astype(f32)
    values = stage[...].astype(bf16)
    col = iota((512, 96), 0)
    comp, corner = (col % 128) // 16, col // 128
    spread = (iota((128, 128), 0) // 16 == iota((128, 128), 1)).astype(bf16)
    same = iota((128, 512), 0) % 16 == iota((128, 512), 1) % 16
    for d in range(4):
        pick = ((comp < 6) & (iota((512, 96), 1) == (comp * 4 + corner) * 4 + d)).astype(bf16)
        by_col = jnp.dot(pick, values, preferred_element_type=f32).astype(bf16)
        block = lax.dot_general(spread, by_col, NT, preferred_element_type=f32)
        weights[d * 128:d * 128 + 128, :] = jnp.where(same, block, 0.0).astype(bf16)


def send_kernel(modes, send_list, order, mass, out0, out1, out2, out3, table, weights,
                near, lists, stage, sem, list_sem):
    nodes = modes.shape[1]
    width = nodes // 4

    def copy(n):
        return pltpu.make_async_copy(modes.at[:, pl.ds(n * width, width)], near.at[:, pl.ds(n * width, width)], sem.at[n])

    for n in range(4):
        copy(n).start()
    list_copy = pltpu.make_async_copy(send_list, lists, list_sem)
    list_copy.start()
    mass_matrix(mass, stage, weights)
    for n in range(4):
        copy(n).wait()

        def transpose(q, _):
            col = pl.ds(pl.multiple_of(n * width + q * TILE, TILE), TILE)
            x = jnp.concatenate([near[:, col].astype(f32), jnp.zeros((32, TILE), f32)], axis=0)
            table[col, :] = x.T
            return 0

        lax.fori_loop(0, width // TILE, transpose, 0, unroll=4)
    list_copy.wait()
    for d, out in enumerate((out0, out1, out2, out3)):
        which = order[d]

        def rows16(s, _):
            rows = [table[pl.ds(lists[which, s * 16 + r], 1), :] for r in range(16)]
            out[pl.ds(pl.multiple_of(s * 16, 16), 16), :] = jnp.concatenate(rows, axis=0).astype(bf16)
            return 0

        lax.fori_loop(0, SLOTS // 16, rows16, 0, unroll=2)


def main_kernel(table_in, ghost0, ghost1, ghost2, ghost3, order, stiff, weights, areas, lam, connect, var,
                own, near, far, table, gather_a, gather_b, f_bufs, s_bufs, u_bufs, mass_rows, masses,
                index_a, index_b, stiff_near, energies, blocks, stiff_sem, index_sem):
    nodes = table_in.shape[0]
    chunks = connect.shape[1] // CHUNK
    gathers, indices = (gather_a, gather_b), (index_a, index_b)

    def stiff_copy(n):
        return pltpu.make_async_copy(
            stiff.at[:, :, :, :, pl.ds(pl.multiple_of(n * TILE, TILE), TILE)], stiff_near.at[n], stiff_sem.at[n])

    def index_copy(n, slot):
        n = jnp.minimum(n, chunks - 1)
        return pltpu.make_async_copy(
            connect.at[:, pl.ds(pl.multiple_of(n * CHUNK, CHUNK), CHUNK)], indices[slot], index_sem.at[slot])

    index_copy(0, 0).start()
    index_copy(1, 1).start()
    for n in range(chunks * TILES):
        stiff_copy(n).start()
    table[0:nodes, :] = table_in[...]
    for d, ghost in enumerate((ghost0, ghost1, ghost2, ghost3)):
        place = pl.multiple_of(nodes + order[d ^ 1] * SLOTS, SLOTS)
        table[pl.ds(place, SLOTS), :] = ghost[...].astype(f32)
    summing = (iota((TILE, TILE), 0) // 32 == iota((TILE, TILE), 1)).astype(bf16)

    def gather_rows(slot, first, last, start=0):
        index, dest = indices[slot], gathers[slot]
        for e in range(first, last):
            for c in range(4):
                dest[c, pl.ds(start + e, 1), :] = table[pl.ds(index[c, start + e], 1), :]

    index_copy(0, 0).wait()
    gather_rows(0, 0, CHUNK)
    index_copy(2, 0).start()

    def prepare(n, q, slot):
        rows, f_buf, s_buf = gathers[slot], f_bufs.at[q], s_bufs.at[q]
        near = stiff_near.at[n * TILES + q].reshape(576, TILE)
        part = slice(q * TILE, (q + 1) * TILE)
        mass = None
        for c in range(4):
            values = rows[c, part, :]
            u_bufs[q, c] = values.T
            term = mass_rows[part, c * 128:(c + 1) * 128] * values
            mass = term if mass is None else mass + term
        mass = mass.T
        masses[q] = sum(mass[k * 16:k * 16 + 16, :] for k in range(1, 6)) + mass[0:16, :]
        for i in range(0, 576, 16):
            f_buf[i:i + 16, :] = near[i:i + 16, :].astype(f32)
        for i in range(24):
            for j in range(i // 8 * 8, 24, 8):
                s_buf[i * 24 + j:i * 24 + j + 8, :] = (
                    f_buf[i * 24 + j:i * 24 + j + 8, :] + f_buf[pl.ds(j * 24 + i, 8, stride=24), :])

    def tile_energy(n, q):
        f_buf, s_buf, u_buf = f_bufs.at[q], s_bufs.at[q], u_bufs.at[q]
        halves = []
        for h in range(2):
            u = [u_buf[c, k * 16 + h * 8:k * 16 + h * 8 + 8, :] for k in range(6) for c in range(4)]
            total = None
            for i in range(24):
                acc = f_buf[i * 25:i * 25 + 1, :] * u[i]
                for j in range(i + 1, 24):
                    acc = acc + s_buf[i * 24 + j:i * 24 + j + 1, :] * u[j]
                total = acc * u[i] if total is None else total + acc * u[i]
            halves.append(total)
        area = areas[pl.ds(n * TILES + q, 1), :]
        energies[n, q] = jnp.concatenate(halves, axis=0) - lam[...] * area * masses[q]

    def add_blocks(n):
        values = jnp.concatenate([pieces(energies[n, q]) for q in range(TILES)], axis=0)
        sums = jnp.dot(values, summing, preferred_element_type=f32)
        for q in range(TILES):
            one = sums[q * 48:q * 48 + 16] + sums[q * 48 + 16:q * 48 + 32] + sums[q * 48 + 32:q * 48 + 48]
            blocks[...] += pltpu.roll(one, n * (CHUNK // 32) + q * 4, 1)

    def body(it, _):
        for slot in range(2):
            n = it * 2 + slot
            index_copy(0, 1 - slot).wait()
            for q in range(TILES):
                stiff_copy(n * TILES + q).wait()

            gather_rows(1 - slot, 0, CHUNK - TILES * BESIDE)
            rows = jnp.concatenate([gathers[slot][c].astype(bf16) for c in range(4)], axis=1)
            mass_rows[...] = jnp.dot(rows, weights[...], preferred_element_type=f32)
            add_blocks((n + chunks - 1) % chunks)
            for q in range(TILES):
                prepare(n, q, slot)

            def one_tile(q, _, n=n, slot=slot):
                tile_energy(n, q)
                if BESIDE:
                    gather_rows(1 - slot, 0, BESIDE, CHUNK - TILES * BESIDE + q * BESIDE)
                return 0

            lax.fori_loop(0, TILES, one_tile, 0)
            index_copy(n + 3, 1 - slot).start()
        return 0

    energies[...] = jnp.zeros_like(energies)
    blocks[...] = jnp.zeros_like(blocks)
    lax.fori_loop(0, chunks // 2, body, 0)
    add_blocks(chunks - 1)
    for slot in range(2):
        index_copy(0, slot).wait()
    columns = (iota((3 * VAR_DEV, 128), 0) == var[...]).astype(bf16)
    window = lax.dot_general(pieces(blocks[...]), columns, NT, preferred_element_type=f32)
    window = window[0:16] + window[16:32] + window[32:48]
    for part, out in enumerate((own, near, far)):
        out[...] = window[:, part * VAR_DEV:(part + 1) * VAR_DEV]


VM = pl.BlockSpec(memory_space=pltpu.VMEM)
SM = pl.BlockSpec(memory_space=pltpu.SMEM)
HB = pl.BlockSpec(memory_space=pltpu.HBM)


def send_rows(modes, send_list, order, mass_ref):
    nodes = modes.shape[1]
    return pl.pallas_call(
        send_kernel,
        out_shape=[jax.ShapeDtypeStruct((SLOTS, 128), bf16)] * 4
        + [jax.ShapeDtypeStruct((nodes, 128), f32), jax.ShapeDtypeStruct((512, 512), bf16)],
        in_specs=[HB, HB, SM, VM], out_specs=[VM] * 6,
        scratch_shapes=[
            pltpu.VMEM(modes.shape, bf16), pltpu.SMEM(send_list.shape, jnp.int32), pltpu.VMEM((96, 128), f32),
            pltpu.SemaphoreType.DMA((4,)), pltpu.SemaphoreType.DMA,
        ],
        compiler_params=pltpu.CompilerParams(vmem_limit_bytes=12 * 2**20),
    )(modes, send_list, order, mass_ref.transpose(0, 1, 3, 2))


def main_call(table, ghosts, order, stiff, weights, areas, lam, connect, var):
    chunks = connect.shape[1] // CHUNK
    return pl.pallas_call(
        main_kernel,
        out_shape=[jax.ShapeDtypeStruct((16, VAR_DEV), f32)] * 3,
        in_specs=[VM, VM, VM, VM, VM, SM, HB, VM, VM, VM, HB, VM], out_specs=[VM] * 3,
        scratch_shapes=[
            pltpu.VMEM((table.shape[0] + 4 * SLOTS, 128), f32),
            pltpu.VMEM((4, CHUNK, 128), f32), pltpu.VMEM((4, CHUNK, 128), f32),
            pltpu.VMEM((TILES, 576, 128), f32), pltpu.VMEM((TILES, 576, 128), f32),
            pltpu.VMEM((TILES, 4, 128, 128), f32), pltpu.VMEM((CHUNK, 512), f32), pltpu.VMEM((TILES, 16, 128), f32),
            pltpu.SMEM((4, CHUNK), jnp.int32), pltpu.SMEM((4, CHUNK), jnp.int32),
            pltpu.VMEM((chunks * TILES, 6, 4, 6, 4, TILE), bf16),
            pltpu.VMEM((chunks, TILES, 16, 128), f32), pltpu.VMEM((16, 128), f32),
            pltpu.SemaphoreType.DMA((chunks * TILES,)), pltpu.SemaphoreType.DMA((2,)),
        ],
        compiler_params=pltpu.CompilerParams(vmem_limit_bytes=57 * 2**20),
    )(table, *ghosts, order, stiff, weights, areas, lam, connect, var)


OFFSETS = (1, -1, 2, -2)


def swap(array, axis, first):
    length = lax.axis_size(axis)
    pairs = []
    for i in range(first, length - 1, 2):
        pairs += [(i, i + 1), (i + 1, i)]
    return lax.ppermute(array, axis, pairs)


def swap_two(array, axis, first):
    length = lax.axis_size(axis)
    pairs = []
    for k in range(2 * first, length - 3, 4):
        for p in range(2):
            pairs += [(k + p, k + p + 2), (k + p + 2, k + p)]
    return lax.ppermute(array, axis, pairs)


def shards(
    modes, stiffness, mass_ref, areas, eigenvalues, send_list, connect, block_var, mode_weight
):
    region = lax.axis_index("region")
    mode_dev, node_count = modes.shape[1:]
    elem_count = connect.shape[1]
    flat = modes.reshape(6 * mode_dev, node_count)
    odd = region % 2
    upper = (region // 2) % 2
    order = jnp.stack([odd, 1 - odd, 2 + upper, 3 - upper]).astype(jnp.int32)
    *sent, table, weights = send_rows(flat, send_list, order, mass_ref)
    received = [swap(sent[0], "region", 0), swap(sent[1], "region", 1),
                swap_two(sent[2], "region", 0), swap_two(sent[3], "region", 1)]
    step = block_var // VAR_DEV - region
    near = jnp.where(odd == 1, -1, 1)
    column = block_var % VAR_DEV + VAR_DEV * jnp.where(step == 0, 0, jnp.where(step == near, 1, 2))
    lam = jnp.broadcast_to(eigenvalues[:, None], (mode_dev, 128))
    own, sent_a, sent_b = main_call(
        table, received, order, stiffness, weights, areas.reshape(elem_count // 128, 128),
        lam, connect, column.reshape(1, 128))
    sens = own + swap(sent_a, "region", 0) + swap(sent_b, "region", 1)
    weighted = jnp.sum(mode_weight[:, None] * sens, axis=0)
    other = [lax.ppermute(weighted, "mode", [(q, q ^ by) for q in range(4)]) for by in (1, 2, 3)]
    weighted = (weighted + other[0]) + (other[1] + other[2])
    return (sens, weighted)


def solution(mesh):
    in_specs = (
        P(None, "mode", "region"),
        P(None, None, None, None, "region"),
        P(),
        P("region"),
        P("mode"),
        P(None, "region"),
        P(None, "region"),
        P("region"),
        P("mode"),
    )
    out_specs = (P("mode", "region"), P("region"))
    return jax.shard_map(shards, mesh=mesh, in_specs=in_specs, out_specs=out_specs, check_vma=False)
```

```python
import jax
import jax.numpy as jnp
from jax import lax
from jax.experimental import pallas as pl
from jax.experimental.pallas import tpu as pltpu
from jax.sharding import PartitionSpec as P

NT = (((1,), (1,)), ((), ()))
SLOTS, VAR_DEV = 128, 128
TILE, CHUNK = 128, 512
TILES = CHUNK // TILE
BESIDE = 0
f32, bf16 = jnp.float32, jnp.bfloat16


def iota(shape, dim):
    return lax.broadcasted_iota(jnp.int32, shape, dim)


def pieces(x):
    hi = x.astype(bf16)
    rest = x - hi.astype(f32)
    mid = rest.astype(bf16)
    low = (rest - mid.astype(f32)).astype(bf16)
    return jnp.concatenate([hi, mid, low], axis=0)


def mass_matrix(mass, stage, weights):
    stage[...] = jnp.zeros_like(stage)
    for a in range(6):
        for c in range(4):
            first = (a * 4 + c) * 4
            stage[first:first + 4, 0:6] = mass[a, c].astype(f32)
    values = stage[...].astype(bf16)
    col = iota((512, 96), 0)
    comp, corner = (col % 128) // 16, col // 128
    spread = (iota((128, 128), 0) // 16 == iota((128, 128), 1)).astype(bf16)
    same = iota((128, 512), 0) % 16 == iota((128, 512), 1) % 16
    for d in range(4):
        pick = ((comp < 6) & (iota((512, 96), 1) == (comp * 4 + corner) * 4 + d)).astype(bf16)
        by_col = jnp.dot(pick, values, preferred_element_type=f32).astype(bf16)
        block = lax.dot_general(spread, by_col, NT, preferred_element_type=f32)
        weights[d * 128:d * 128 + 128, :] = jnp.where(same, block, 0.0).astype(bf16)


def fill_table(modes, table):
    def transpose(q, _):
        col = pl.ds(pl.multiple_of(q * TILE, TILE), TILE)
        x = jnp.concatenate([modes[:, col].astype(f32), jnp.zeros((32, TILE), f32)], axis=0)
        table[col, :] = x.T
        return 0

    lax.fori_loop(0, modes.shape[1] // TILE, transpose, 0, unroll=8)


def send_kernel(modes, send_list, order, out0, out1, out2, out3, table):
    fill_table(modes, table)
    for d, out in enumerate((out0, out1, out2, out3)):
        which = order[d]

        def rows16(s, _):
            rows = [table[pl.ds(send_list[which, s * 16 + r], 1), :] for r in range(16)]
            out[pl.ds(pl.multiple_of(s * 16, 16), 16), :] = jnp.concatenate(rows, axis=0).astype(bf16)
            return 0

        lax.fori_loop(0, SLOTS // 16, rows16, 0, unroll=2)


def main_kernel(modes, ghost0, ghost1, ghost2, ghost3, order, stiff, mass_ref, areas, eigenvalues, connect, variables,
                own, near, far, stage, weights, lam, table, gather_a, gather_b, f_bufs, s_bufs, u_bufs, mass_rows, masses,
                index_a, index_b, stiff_near, energies, blocks, stiff_sem, index_sem):
    nodes = modes.shape[1]
    chunks = connect.shape[1] // CHUNK
    gathers, indices = (gather_a, gather_b), (index_a, index_b)

    def stiff_copy(n):
        return pltpu.make_async_copy(
            stiff.at[:, :, :, :, pl.ds(pl.multiple_of(n * TILE, TILE), TILE)], stiff_near.at[n], stiff_sem.at[n])

    def index_copy(n, slot):
        n = jnp.minimum(n, chunks - 1)
        return pltpu.make_async_copy(
            connect.at[:, pl.ds(pl.multiple_of(n * CHUNK, CHUNK), CHUNK)], indices[slot], index_sem.at[slot])

    index_copy(0, 0).start()
    index_copy(1, 1).start()
    for n in range(chunks * TILES):
        stiff_copy(n).start()
    mass_matrix(mass_ref, stage, weights)
    row = iota((16, 128), 0)
    scale = jnp.zeros((16, 128), f32)
    for m in range(16):
        scale = jnp.where(row == m, eigenvalues[m], scale)
    lam[...] = scale
    fill_table(modes, table)
    for d, ghost in enumerate((ghost0, ghost1, ghost2, ghost3)):
        place = pl.multiple_of(nodes + order[d ^ 1] * SLOTS, SLOTS)
        table[pl.ds(place, SLOTS), :] = ghost[...].astype(f32)
    summing = (iota((TILE, TILE), 0) // 32 == iota((TILE, TILE), 1)).astype(bf16)

    def gather_rows(slot, first, last, start=0):
        index, dest = indices[slot], gathers[slot]
        for e in range(first, last):
            for c in range(4):
                dest[c, pl.ds(start + e, 1), :] = table[pl.ds(index[c, start + e], 1), :]

    index_copy(0, 0).wait()
    gather_rows(0, 0, CHUNK)
    index_copy(2, 0).start()

    def prepare(n, q, slot):
        rows, f_buf, s_buf = gathers[slot], f_bufs.at[q], s_bufs.at[q]
        near = stiff_near.at[n * TILES + q].reshape(576, TILE)
        part = slice(q * TILE, (q + 1) * TILE)
        mass = None
        for c in range(4):
            values = rows[c, part, :]
            u_bufs[q, c] = values.T
            term = mass_rows[part, c * 128:(c + 1) * 128] * values
            mass = term if mass is None else mass + term
        mass = mass.T
        masses[q] = sum(mass[k * 16:k * 16 + 16, :] for k in range(1, 6)) + mass[0:16, :]
        for i in range(0, 576, 16):
            f_buf[i:i + 16, :] = near[i:i + 16, :].astype(f32)
        for i in range(24):
            for j in range(i // 8 * 8, 24, 8):
                s_buf[i * 24 + j:i * 24 + j + 8, :] = (
                    f_buf[i * 24 + j:i * 24 + j + 8, :] + f_buf[pl.ds(j * 24 + i, 8, stride=24), :])

    def tile_energy(n, q):
        f_buf, s_buf, u_buf = f_bufs.at[q], s_bufs.at[q], u_bufs.at[q]
        halves = []
        for h in range(2):
            u = [u_buf[c, k * 16 + h * 8:k * 16 + h * 8 + 8, :] for k in range(6) for c in range(4)]
            total = None
            for i in range(24):
                acc = f_buf[i * 25:i * 25 + 1, :] * u[i]
                for j in range(i + 1, 24):
                    acc = acc + s_buf[i * 24 + j:i * 24 + j + 1, :] * u[j]
                total = acc * u[i] if total is None else total + acc * u[i]
            halves.append(total)
        area = areas[pl.ds(n * TILES + q, 1), :]
        energies[n, q] = jnp.concatenate(halves, axis=0) - lam[...] * area * masses[q]

    def add_blocks(n):
        values = jnp.concatenate([pieces(energies[n, q]) for q in range(TILES)], axis=0)
        sums = jnp.dot(values, summing, preferred_element_type=f32)
        for q in range(TILES):
            one = sums[q * 48:q * 48 + 16] + sums[q * 48 + 16:q * 48 + 32] + sums[q * 48 + 32:q * 48 + 48]
            blocks[...] += pltpu.roll(one, n * (CHUNK // 32) + q * 4, 1)

    def body(it, _):
        for slot in range(2):
            n = it * 2 + slot
            index_copy(0, 1 - slot).wait()
            for q in range(TILES):
                stiff_copy(n * TILES + q).wait()

            gather_rows(1 - slot, 0, CHUNK - TILES * BESIDE)
            rows = jnp.concatenate([gathers[slot][c].astype(bf16) for c in range(4)], axis=1)
            mass_rows[...] = jnp.dot(rows, weights[...], preferred_element_type=f32)
            add_blocks((n + chunks - 1) % chunks)
            for q in range(TILES):
                prepare(n, q, slot)

            def one_tile(q, _, n=n, slot=slot):
                tile_energy(n, q)
                if BESIDE:
                    gather_rows(1 - slot, 0, BESIDE, CHUNK - TILES * BESIDE + q * BESIDE)
                return 0

            lax.fori_loop(0, TILES, one_tile, 0)
            index_copy(n + 3, 1 - slot).start()
        return 0

    energies[...] = jnp.zeros_like(energies)
    blocks[...] = jnp.zeros_like(blocks)
    lax.fori_loop(0, chunks // 2, body, 0)
    add_blocks(chunks - 1)
    for slot in range(2):
        index_copy(0, slot).wait()
    step = variables[...] // VAR_DEV - order[4]
    place = jnp.where(step == 0, 0, jnp.where(step == 1 - 2 * order[0], 1, 2))
    var = variables[...] % VAR_DEV + VAR_DEV * place
    columns = (iota((3 * VAR_DEV, 128), 0) == var).astype(bf16)
    window = lax.dot_general(pieces(blocks[...]), columns, NT, preferred_element_type=f32)
    window = window[0:16] + window[16:32] + window[32:48]
    for part, out in enumerate((own, near, far)):
        out[...] = window[:, part * VAR_DEV:(part + 1) * VAR_DEV]


VM = pl.BlockSpec(memory_space=pltpu.VMEM)
SM = pl.BlockSpec(memory_space=pltpu.SMEM)
HB = pl.BlockSpec(memory_space=pltpu.HBM)


def send_rows(modes, send_list, order):
    return pl.pallas_call(
        send_kernel,
        out_shape=[jax.ShapeDtypeStruct((SLOTS, 128), bf16)] * 4,
        in_specs=[VM, SM, SM], out_specs=[VM] * 4,
        scratch_shapes=[pltpu.VMEM((modes.shape[1], 128), f32)],
        compiler_params=pltpu.CompilerParams(vmem_limit_bytes=12 * 2**20),
    )(modes, send_list, order)


def main_call(modes, ghosts, order, stiff, mass_ref, areas, eigenvalues, connect, variables):
    chunks = connect.shape[1] // CHUNK
    return pl.pallas_call(
        main_kernel,
        out_shape=[jax.ShapeDtypeStruct((16, VAR_DEV), f32)] * 3,
        in_specs=[VM, VM, VM, VM, VM, SM, HB, VM, VM, SM, HB, VM], out_specs=[VM] * 3,
        scratch_shapes=[
            pltpu.VMEM((96, 128), f32), pltpu.VMEM((512, 512), bf16), pltpu.VMEM((16, 128), f32),
            pltpu.VMEM((modes.shape[1] + 4 * SLOTS, 128), f32),
            pltpu.VMEM((4, CHUNK, 128), f32), pltpu.VMEM((4, CHUNK, 128), f32),
            pltpu.VMEM((TILES, 576, 128), f32), pltpu.VMEM((TILES, 576, 128), f32),
            pltpu.VMEM((TILES, 4, 128, 128), f32), pltpu.VMEM((CHUNK, 512), f32), pltpu.VMEM((TILES, 16, 128), f32),
            pltpu.SMEM((4, CHUNK), jnp.int32), pltpu.SMEM((4, CHUNK), jnp.int32),
            pltpu.VMEM((chunks * TILES, 6, 4, 6, 4, TILE), bf16),
            pltpu.VMEM((chunks, TILES, 16, 128), f32), pltpu.VMEM((16, 128), f32),
            pltpu.SemaphoreType.DMA((chunks * TILES,)), pltpu.SemaphoreType.DMA((2,)),
        ],
        compiler_params=pltpu.CompilerParams(vmem_limit_bytes=57 * 2**20),
    )(modes, *ghosts, order, stiff, mass_ref.transpose(0, 1, 3, 2), areas, eigenvalues, connect, variables)


OFFSETS = (1, -1, 2, -2)


def swap(array, axis, first):
    length = lax.axis_size(axis)
    pairs = []
    for i in range(first, length - 1, 2):
        pairs += [(i, i + 1), (i + 1, i)]
    return lax.ppermute(array, axis, pairs)


def swap_two(array, axis, first):
    length = lax.axis_size(axis)
    pairs = []
    for k in range(2 * first, length - 3, 4):
        for p in range(2):
            pairs += [(k + p, k + p + 2), (k + p + 2, k + p)]
    return lax.ppermute(array, axis, pairs)


def shards(
    modes, stiffness, mass_ref, areas, eigenvalues, send_list, connect, block_var, mode_weight
):
    region = lax.axis_index("region")
    mode_dev, node_count = modes.shape[1:]
    elem_count = connect.shape[1]
    flat = modes.reshape(6 * mode_dev, node_count)
    odd = region % 2
    upper = (region // 2) % 2
    order = jnp.stack([odd, 1 - odd, 2 + upper, 3 - upper, region]).astype(jnp.int32)
    sent = send_rows(flat, send_list, order)
    received = [swap(sent[0], "region", 0), swap(sent[1], "region", 1),
                swap_two(sent[2], "region", 0), swap_two(sent[3], "region", 1)]
    own, sent_a, sent_b = main_call(
        flat, received, order, stiffness, mass_ref, areas.reshape(elem_count // 128, 128),
        eigenvalues, connect, block_var.reshape(1, elem_count // 32))
    sens = own + swap(sent_a, "region", 0) + swap(sent_b, "region", 1)
    weighted = jnp.sum(mode_weight[:, None] * sens, axis=0)
    other = [lax.ppermute(weighted, "mode", [(q, q ^ by) for q in range(4)]) for by in (1, 2, 3)]
    weighted = (weighted + other[0]) + (other[1] + other[2])
    return (sens, weighted)


def solution(mesh):
    in_specs = (
        P(None, "mode", "region"),
        P(None, None, None, None, "region"),
        P(),
        P("region"),
        P("mode"),
        P(None, "region"),
        P(None, "region"),
        P("region"),
        P("mode"),
    )
    out_specs = (P("mode", "region"), P("region"))
    return jax.shard_map(shards, mesh=mesh, in_specs=in_specs, out_specs=out_specs, check_vma=False)
```

```python
import jax
import jax.numpy as jnp
from jax import lax
from jax.experimental import pallas as pl
from jax.experimental.pallas import tpu as pltpu
from jax.sharding import PartitionSpec as P

NT = (((1,), (1,)), ((), ()))
SLOTS, VAR_DEV = 128, 128
TILE, CHUNK = 128, 512
TILES = CHUNK // TILE
BESIDE = 0
f32, bf16 = jnp.float32, jnp.bfloat16


def iota(shape, dim):
    return lax.broadcasted_iota(jnp.int32, shape, dim)


def pieces(x):
    hi = x.astype(bf16)
    rest = x - hi.astype(f32)
    mid = rest.astype(bf16)
    low = (rest - mid.astype(f32)).astype(bf16)
    return jnp.concatenate([hi, mid, low], axis=0)


def mass_matrix(mass, stage, weights):
    stage[...] = jnp.zeros_like(stage)
    for a in range(6):
        for c in range(4):
            first = (a * 4 + c) * 4
            stage[first:first + 4, 0:6] = mass[a, c]
    values = stage[...].astype(bf16)
    col = iota((512, 96), 0)
    comp, corner = (col % 128) // 16, col // 128
    spread = (iota((128, 128), 0) // 16 == iota((128, 128), 1)).astype(bf16)
    same = iota((128, 512), 0) % 16 == iota((128, 512), 1) % 16
    for d in range(4):
        pick = ((comp < 6) & (iota((512, 96), 1) == (comp * 4 + corner) * 4 + d)).astype(bf16)
        by_col = jnp.dot(pick, values, preferred_element_type=f32).astype(bf16)
        block = lax.dot_general(spread, by_col, NT, preferred_element_type=f32)
        weights[d * 128:d * 128 + 128, :] = jnp.where(same, block, 0.0).astype(bf16)


def fill_table(modes, table):
    def transpose(q, _):
        col = pl.ds(pl.multiple_of(q * TILE, TILE), TILE)
        x = jnp.concatenate([modes[:, col].astype(f32), jnp.zeros((32, TILE), f32)], axis=0)
        table[col, :] = x.T
        return 0

    lax.fori_loop(0, modes.shape[1] // TILE, transpose, 0, unroll=8)


def send_kernel(modes, send_list, order, out0, out1, out2, out3, table):
    fill_table(modes, table)
    for d, out in enumerate((out0, out1, out2, out3)):
        which = order[d]

        def rows16(s, _):
            rows = [table[pl.ds(send_list[which, s * 16 + r], 1), :] for r in range(16)]
            out[pl.ds(pl.multiple_of(s * 16, 16), 16), :] = jnp.concatenate(rows, axis=0).astype(bf16)
            return 0

        lax.fori_loop(0, SLOTS // 16, rows16, 0, unroll=2)


def main_kernel(rows_in, ghost0, ghost1, ghost2, ghost3, order, stiff, mass_ref, minus_areas, lam, connect, var,
                own, near, far, stage, weights, table, gather_a, gather_b, f_bufs, s_bufs, u_bufs, mass_rows, masses,
                index_a, index_b, stiff_near, energies, blocks, stiff_sem, index_sem):
    nodes = rows_in.shape[0]
    chunks = connect.shape[1] // CHUNK
    gathers, indices = (gather_a, gather_b), (index_a, index_b)

    def stiff_copy(n):
        return pltpu.make_async_copy(
            stiff.at[:, :, :, :, pl.ds(pl.multiple_of(n * TILE, TILE), TILE)], stiff_near.at[n], stiff_sem.at[n])

    def index_copy(n, slot):
        n = jnp.minimum(n, chunks - 1)
        return pltpu.make_async_copy(
            connect.at[:, pl.ds(pl.multiple_of(n * CHUNK, CHUNK), CHUNK)], indices[slot], index_sem.at[slot])

    index_copy(0, 0).start()
    index_copy(1, 1).start()
    for n in range(chunks * TILES):
        stiff_copy(n).start()
    mass_matrix(mass_ref, stage, weights)
    table[0:nodes, :] = rows_in[...]
    for d, ghost in enumerate((ghost0, ghost1, ghost2, ghost3)):
        place = pl.multiple_of(nodes + order[d ^ 1] * SLOTS, SLOTS)
        table[pl.ds(place, SLOTS), :] = ghost[...].astype(f32)
    summing = (iota((TILE, TILE), 0) // 32 == iota((TILE, TILE), 1)).astype(bf16)

    def gather_rows(slot, first, last, start=0):
        index, dest = indices[slot], gathers[slot]
        for e in range(first, last):
            for c in range(4):
                dest[c, pl.ds(start + e, 1), :] = table[pl.ds(index[c, start + e], 1), :]

    index_copy(0, 0).wait()
    gather_rows(0, 0, CHUNK)
    index_copy(2, 0).start()

    def prepare(n, q, slot):
        rows, f_buf, s_buf = gathers[slot], f_bufs.at[q], s_bufs.at[q]
        near = stiff_near.at[n * TILES + q].reshape(576, TILE)
        part = slice(q * TILE, (q + 1) * TILE)
        mass = None
        for c in range(4):
            values = rows[c, part, :]
            u_bufs[q, c] = values.T
            term = mass_rows[part, c * 128:(c + 1) * 128] * values
            mass = term if mass is None else mass + term
        mass = mass.T
        masses[q] = sum(mass[k * 16:k * 16 + 16, :] for k in range(1, 6)) + mass[0:16, :]
        for i in range(0, 576, 16):
            f_buf[i:i + 16, :] = near[i:i + 16, :].astype(f32)
        for i in range(24):
            for j in range(i // 8 * 8, 24, 8):
                s_buf[i * 24 + j:i * 24 + j + 8, :] = (
                    f_buf[i * 24 + j:i * 24 + j + 8, :] + f_buf[pl.ds(j * 24 + i, 8, stride=24), :])

    def tile_energy(n, q):
        f_buf, s_buf, u_buf = f_bufs.at[q], s_bufs.at[q], u_bufs.at[q]
        halves = []
        for h in range(2):
            u = [u_buf[c, k * 16 + h * 8:k * 16 + h * 8 + 8, :] for k in range(6) for c in range(4)]
            total = None
            for i in range(24):
                acc = f_buf[i * 25:i * 25 + 1, :] * u[i]
                for j in range(i + 1, 24):
                    acc = acc + s_buf[i * 24 + j:i * 24 + j + 1, :] * u[j]
                total = acc * u[i] if total is None else total + acc * u[i]
            halves.append(total)
        area = minus_areas[pl.ds(n * TILES + q, 1), :]
        energies[n, q] = jnp.concatenate(halves, axis=0) + lam[...] * area * masses[q]

    def add_blocks(n):
        values = jnp.concatenate([pieces(energies[n, q]) for q in range(TILES)], axis=0)
        sums = jnp.dot(values, summing, preferred_element_type=f32)
        for q in range(TILES):
            one = sums[q * 48:q * 48 + 16] + sums[q * 48 + 16:q * 48 + 32] + sums[q * 48 + 32:q * 48 + 48]
            blocks[...] += pltpu.roll(one, n * (CHUNK // 32) + q * 4, 1)

    def body(it, _):
        for slot in range(2):
            n = it * 2 + slot
            index_copy(0, 1 - slot).wait()
            for q in range(TILES):
                stiff_copy(n * TILES + q).wait()

            gather_rows(1 - slot, 0, CHUNK - TILES * BESIDE)
            rows = jnp.concatenate([gathers[slot][c].astype(bf16) for c in range(4)], axis=1)
            mass_rows[...] = jnp.dot(rows, weights[...], preferred_element_type=f32)
            add_blocks((n + chunks - 1) % chunks)
            for q in range(TILES):
                prepare(n, q, slot)

            def one_tile(q, _, n=n, slot=slot):
                tile_energy(n, q)
                if BESIDE:
                    gather_rows(1 - slot, 0, BESIDE, CHUNK - TILES * BESIDE + q * BESIDE)
                return 0

            lax.fori_loop(0, TILES, one_tile, 0)
            index_copy(n + 3, 1 - slot).start()
        return 0

    energies[...] = jnp.zeros_like(energies)
    blocks[...] = jnp.zeros_like(blocks)
    lax.fori_loop(0, chunks // 2, body, 0)
    add_blocks(chunks - 1)
    for slot in range(2):
        index_copy(0, slot).wait()
    columns = (iota((3 * VAR_DEV, 128), 0) == var[...]).astype(bf16)
    window = lax.dot_general(pieces(blocks[...]), columns, NT, preferred_element_type=f32)
    window = window[0:16] + window[16:32] + window[32:48]
    for part, out in enumerate((own, near, far)):
        out[...] = window[:, part * VAR_DEV:(part + 1) * VAR_DEV]


VM = pl.BlockSpec(memory_space=pltpu.VMEM)
SM = pl.BlockSpec(memory_space=pltpu.SMEM)
HB = pl.BlockSpec(memory_space=pltpu.HBM)


def send_rows(modes, send_list, order):
    return pl.pallas_call(
        send_kernel,
        out_shape=[jax.ShapeDtypeStruct((SLOTS, 128), bf16)] * 4 + [jax.ShapeDtypeStruct((modes.shape[1], 128), f32)],
        in_specs=[VM, SM, SM], out_specs=[VM] * 5,
        compiler_params=pltpu.CompilerParams(vmem_limit_bytes=12 * 2**20),
    )(modes, send_list, order)


def main_call(rows, ghosts, order, stiff, mass_ref, minus_areas, lam, connect, var):
    chunks = connect.shape[1] // CHUNK
    return pl.pallas_call(
        main_kernel,
        out_shape=[jax.ShapeDtypeStruct((16, VAR_DEV), f32)] * 3,
        in_specs=[VM, VM, VM, VM, VM, SM, HB, VM, VM, VM, HB, VM], out_specs=[VM] * 3,
        scratch_shapes=[
            pltpu.VMEM((96, 128), f32), pltpu.VMEM((512, 512), bf16),
            pltpu.VMEM((rows.shape[0] + 4 * SLOTS, 128), f32),
            pltpu.VMEM((4, CHUNK, 128), f32), pltpu.VMEM((4, CHUNK, 128), f32),
            pltpu.VMEM((TILES, 576, 128), f32), pltpu.VMEM((TILES, 576, 128), f32),
            pltpu.VMEM((TILES, 4, 128, 128), f32), pltpu.VMEM((CHUNK, 512), f32), pltpu.VMEM((TILES, 16, 128), f32),
            pltpu.SMEM((4, CHUNK), jnp.int32), pltpu.SMEM((4, CHUNK), jnp.int32),
            pltpu.VMEM((chunks * TILES, 6, 4, 6, 4, TILE), bf16),
            pltpu.VMEM((chunks, TILES, 16, 128), f32), pltpu.VMEM((16, 128), f32),
            pltpu.SemaphoreType.DMA((chunks * TILES,)), pltpu.SemaphoreType.DMA((2,)),
        ],
        compiler_params=pltpu.CompilerParams(vmem_limit_bytes=50 * 2**20),
    )(rows, *ghosts, order, stiff, mass_ref, minus_areas, lam, connect, var)


OFFSETS = (1, -1, 2, -2)


def swap(array, axis, first):
    length = lax.axis_size(axis)
    pairs = []
    for i in range(first, length - 1, 2):
        pairs += [(i, i + 1), (i + 1, i)]
    return lax.ppermute(array, axis, pairs)


def swap_two(array, axis, first):
    length = lax.axis_size(axis)
    pairs = []
    for k in range(2 * first, length - 3, 4):
        for p in range(2):
            pairs += [(k + p, k + p + 2), (k + p + 2, k + p)]
    return lax.ppermute(array, axis, pairs)


def shards(
    modes, stiffness, mass_ref, areas, eigenvalues, send_list, connect, block_var, mode_weight
):
    region = lax.axis_index("region")
    mode_dev, node_count = modes.shape[1:]
    elem_count = connect.shape[1]
    flat = modes.reshape(6 * mode_dev, node_count)
    odd = region % 2
    upper = (region // 2) % 2
    order = jnp.stack([odd, 1 - odd, 2 + upper, 3 - upper]).astype(jnp.int32)
    *sent, rows = send_rows(flat, send_list, order)
    received = [swap(sent[0], "region", 0), swap(sent[1], "region", 1),
                swap_two(sent[2], "region", 0), swap_two(sent[3], "region", 1)]
    step = block_var // VAR_DEV - region
    place = jnp.where(step == 0, 0, jnp.where(step == 1 - 2 * odd, 1, 2))
    column = block_var % VAR_DEV + VAR_DEV * place
    own, sent_a, sent_b = main_call(
        rows, received, order, stiffness, mass_ref.transpose(0, 1, 3, 2).astype(f32),
        -areas.reshape(elem_count // 128, 128), jnp.broadcast_to(eigenvalues[:, None], (mode_dev, 128)),
        jnp.minimum(connect, node_count + 4 * SLOTS - 1), column.reshape(1, elem_count // 32))
    sens = own + swap(sent_a, "region", 0) + swap(sent_b, "region", 1)
    weighted = jnp.sum(mode_weight[:, None] * sens, axis=0)
    other = [lax.ppermute(weighted, "mode", [(q, q ^ by) for q in range(4)]) for by in (1, 2, 3)]
    weighted = (weighted + other[0]) + (other[1] + other[2])
    return (sens, weighted)


def solution(mesh):
    in_specs = (
        P(None, "mode", "region"),
        P(None, None, None, None, "region"),
        P(),
        P("region"),
        P("mode"),
        P(None, "region"),
        P(None, "region"),
        P("region"),
        P("mode"),
    )
    out_specs = (P("mode", "region"), P("region"))
    return jax.shard_map(shards, mesh=mesh, in_specs=in_specs, out_specs=out_specs, check_vma=False)
```

```python
import jax
import jax.numpy as jnp
from jax import lax
from jax.experimental import pallas as pl
from jax.experimental.pallas import tpu as pltpu
from jax.sharding import PartitionSpec as P

NT = (((1,), (1,)), ((), ()))
SLOTS, VAR_DEV = 128, 128
TILE, CHUNK = 128, 512
TILES = CHUNK // TILE
BESIDE = 0
f32, bf16 = jnp.float32, jnp.bfloat16


def iota(shape, dim):
    return lax.broadcasted_iota(jnp.int32, shape, dim)


def pieces(x):
    hi = x.astype(bf16)
    rest = x - hi.astype(f32)
    mid = rest.astype(bf16)
    low = (rest - mid.astype(f32)).astype(bf16)
    return jnp.concatenate([hi, mid, low], axis=0)


def mass_matrix(mass, stage, weights):
    stage[...] = jnp.zeros_like(stage)
    for a in range(6):
        for c in range(4):
            first = (a * 4 + c) * 4
            stage[first:first + 4, 0:6] = mass[a, c]
    values = stage[...].astype(bf16)
    col = iota((512, 96), 0)
    comp, corner = (col % 128) // 16, col // 128
    spread = (iota((128, 128), 0) // 16 == iota((128, 128), 1)).astype(bf16)
    same = iota((128, 512), 0) % 16 == iota((128, 512), 1) % 16
    for d in range(4):
        pick = ((comp < 6) & (iota((512, 96), 1) == (comp * 4 + corner) * 4 + d)).astype(bf16)
        by_col = jnp.dot(pick, values, preferred_element_type=f32).astype(bf16)
        block = lax.dot_general(spread, by_col, NT, preferred_element_type=f32)
        weights[d * 128:d * 128 + 128, :] = jnp.where(same, block, 0.0).astype(bf16)


def fill_table(modes, table):
    def transpose(q, _):
        col = pl.ds(pl.multiple_of(q * TILE, TILE), TILE)
        x = jnp.concatenate([modes[:, col].astype(f32), jnp.zeros((32, TILE), f32)], axis=0)
        table[col, :] = x.T
        return 0

    lax.fori_loop(0, modes.shape[1] // TILE, transpose, 0, unroll=8)


def send_kernel(modes, send_list, order, out0, out1, out2, out3, table):
    fill_table(modes, table)
    for d, out in enumerate((out0, out1, out2, out3)):
        which = order[d]

        def rows16(s, _):
            rows = [table[pl.ds(send_list[which, s * 16 + r], 1), :] for r in range(16)]
            out[pl.ds(pl.multiple_of(s * 16, 16), 16), :] = jnp.concatenate(rows, axis=0).astype(bf16)
            return 0

        lax.fori_loop(0, SLOTS // 16, rows16, 0, unroll=2)


def main_kernel(rows_in, ghost0, ghost1, ghost2, ghost3, order, stiff, mass_ref, factors, connect,
                own, near, far, stage, weights, table, gather_a, gather_b, f_bufs, s_bufs, u_bufs, mass_rows, masses,
                index_a, index_b, stiff_near, energies, blocks, stiff_sem, index_sem):
    nodes = rows_in.shape[0]
    chunks = connect.shape[1] // CHUNK
    gathers, indices = (gather_a, gather_b), (index_a, index_b)

    def stiff_copy(n):
        return pltpu.make_async_copy(
            stiff.at[:, :, :, :, pl.ds(pl.multiple_of(n * TILE, TILE), TILE)], stiff_near.at[n], stiff_sem.at[n])

    def index_copy(n, slot):
        n = jnp.minimum(n, chunks - 1)
        return pltpu.make_async_copy(
            connect.at[:, pl.ds(pl.multiple_of(n * CHUNK, CHUNK), CHUNK)], indices[slot], index_sem.at[slot])

    index_copy(0, 0).start()
    index_copy(1, 1).start()
    for n in range(chunks * TILES):
        stiff_copy(n).start()
    mass_matrix(mass_ref, stage, weights)
    table[0:nodes, :] = rows_in[...]
    for d, ghost in enumerate((ghost0, ghost1, ghost2, ghost3)):
        place = pl.multiple_of(nodes + order[d ^ 1] * SLOTS, SLOTS)
        table[pl.ds(place, SLOTS), :] = ghost[...].astype(f32)
    summing = (iota((TILE, TILE), 0) // 32 == iota((TILE, TILE), 1)).astype(bf16)

    def gather_rows(slot, first, last, start=0):
        index, dest = indices[slot], gathers[slot]
        for e in range(first, last):
            for c in range(4):
                dest[c, pl.ds(start + e, 1), :] = table[pl.ds(index[c, start + e], 1), :]

    index_copy(0, 0).wait()
    gather_rows(0, 0, CHUNK)
    index_copy(2, 0).start()

    def prepare(n, q, slot):
        rows, f_buf, s_buf = gathers[slot], f_bufs.at[q], s_bufs.at[q]
        near = stiff_near.at[n * TILES + q].reshape(576, TILE)
        part = slice(q * TILE, (q + 1) * TILE)
        mass = None
        for c in range(4):
            values = rows[c, part, :]
            u_bufs[q, c] = values.T
            term = mass_rows[part, c * 128:(c + 1) * 128] * values
            mass = term if mass is None else mass + term
        mass = mass.T
        masses[q] = sum(mass[k * 16:k * 16 + 16, :] for k in range(1, 6)) + mass[0:16, :]
        for i in range(0, 576, 16):
            f_buf[i:i + 16, :] = near[i:i + 16, :].astype(f32)
        for i in range(24):
            for j in range(i // 8 * 8, 24, 8):
                s_buf[i * 24 + j:i * 24 + j + 8, :] = (
                    f_buf[i * 24 + j:i * 24 + j + 8, :] + f_buf[pl.ds(j * 24 + i, 8, stride=24), :])

    def tile_energy(n, q):
        f_buf, s_buf, u_buf = f_bufs.at[q], s_bufs.at[q], u_bufs.at[q]
        halves = []
        for h in range(2):
            u = [u_buf[c, k * 16 + h * 8:k * 16 + h * 8 + 8, :] for k in range(6) for c in range(4)]
            total = None
            for i in range(24):
                acc = f_buf[i * 25:i * 25 + 1, :] * u[i]
                for j in range(i + 1, 24):
                    acc = acc + s_buf[i * 24 + j:i * 24 + j + 1, :] * u[j]
                total = acc * u[i] if total is None else total + acc * u[i]
            halves.append(total)
        area = factors[pl.ds(16 + n * TILES + q, 1), :]
        energies[n, q] = jnp.concatenate(halves, axis=0) + factors[0:16, :] * area * masses[q]

    def add_blocks(n):
        values = jnp.concatenate([pieces(energies[n, q]) for q in range(TILES)], axis=0)
        sums = jnp.dot(values, summing, preferred_element_type=f32)
        for q in range(TILES):
            one = sums[q * 48:q * 48 + 16] + sums[q * 48 + 16:q * 48 + 32] + sums[q * 48 + 32:q * 48 + 48]
            blocks[...] += pltpu.roll(one, n * (CHUNK // 32) + q * 4, 1)

    def body(it, _):
        for slot in range(2):
            n = it * 2 + slot
            index_copy(0, 1 - slot).wait()
            for q in range(TILES):
                stiff_copy(n * TILES + q).wait()

            gather_rows(1 - slot, 0, CHUNK - TILES * BESIDE)
            rows = jnp.concatenate([gathers[slot][c].astype(bf16) for c in range(4)], axis=1)
            mass_rows[...] = jnp.dot(rows, weights[...], preferred_element_type=f32)
            add_blocks((n + chunks - 1) % chunks)
            for q in range(TILES):
                prepare(n, q, slot)

            def one_tile(q, _, n=n, slot=slot):
                tile_energy(n, q)
                if BESIDE:
                    gather_rows(1 - slot, 0, BESIDE, CHUNK - TILES * BESIDE + q * BESIDE)
                return 0

            lax.fori_loop(0, TILES, one_tile, 0)
            index_copy(n + 3, 1 - slot).start()
        return 0

    energies[...] = jnp.zeros_like(energies)
    blocks[...] = jnp.zeros_like(blocks)
    lax.fori_loop(0, chunks // 2, body, 0)
    add_blocks(chunks - 1)
    for slot in range(2):
        index_copy(0, slot).wait()
    columns = (iota((3 * VAR_DEV, 128), 0) == factors[16 + chunks * TILES:17 + chunks * TILES, :].astype(jnp.int32)).astype(bf16)
    window = lax.dot_general(pieces(blocks[...]), columns, NT, preferred_element_type=f32)
    window = window[0:16] + window[16:32] + window[32:48]
    for part, out in enumerate((own, near, far)):
        out[...] = window[:, part * VAR_DEV:(part + 1) * VAR_DEV]


VM = pl.BlockSpec(memory_space=pltpu.VMEM)
SM = pl.BlockSpec(memory_space=pltpu.SMEM)
HB = pl.BlockSpec(memory_space=pltpu.HBM)


def send_rows(modes, send_list, order):
    return pl.pallas_call(
        send_kernel,
        out_shape=[jax.ShapeDtypeStruct((SLOTS, 128), bf16)] * 4 + [jax.ShapeDtypeStruct((modes.shape[1], 128), f32)],
        in_specs=[VM, SM, SM], out_specs=[VM] * 5,
        compiler_params=pltpu.CompilerParams(vmem_limit_bytes=12 * 2**20),
    )(modes, send_list, order)


def main_call(rows, ghosts, order, stiff, mass_ref, factors, connect):
    chunks = connect.shape[1] // CHUNK
    return pl.pallas_call(
        main_kernel,
        out_shape=[jax.ShapeDtypeStruct((16, VAR_DEV), f32)] * 3,
        in_specs=[VM, VM, VM, VM, VM, SM, HB, VM, VM, HB], out_specs=[VM] * 3,
        scratch_shapes=[
            pltpu.VMEM((96, 128), f32), pltpu.VMEM((512, 512), bf16),
            pltpu.VMEM((rows.shape[0] + 4 * SLOTS, 128), f32),
            pltpu.VMEM((4, CHUNK, 128), f32), pltpu.VMEM((4, CHUNK, 128), f32),
            pltpu.VMEM((TILES, 576, 128), f32), pltpu.VMEM((TILES, 576, 128), f32),
            pltpu.VMEM((TILES, 4, 128, 128), f32), pltpu.VMEM((CHUNK, 512), f32), pltpu.VMEM((TILES, 16, 128), f32),
            pltpu.SMEM((4, CHUNK), jnp.int32), pltpu.SMEM((4, CHUNK), jnp.int32),
            pltpu.VMEM((chunks * TILES, 6, 4, 6, 4, TILE), bf16),
            pltpu.VMEM((chunks, TILES, 16, 128), f32), pltpu.VMEM((16, 128), f32),
            pltpu.SemaphoreType.DMA((chunks * TILES,)), pltpu.SemaphoreType.DMA((2,)),
        ],
        compiler_params=pltpu.CompilerParams(vmem_limit_bytes=50 * 2**20),
    )(rows, *ghosts, order, stiff, mass_ref, factors, connect)


OFFSETS = (1, -1, 2, -2)


def swap(array, axis, first):
    length = lax.axis_size(axis)
    pairs = []
    for i in range(first, length - 1, 2):
        pairs += [(i, i + 1), (i + 1, i)]
    return lax.ppermute(array, axis, pairs)


def swap_two(array, axis, first):
    length = lax.axis_size(axis)
    pairs = []
    for k in range(2 * first, length - 3, 4):
        for p in range(2):
            pairs += [(k + p, k + p + 2), (k + p + 2, k + p)]
    return lax.ppermute(array, axis, pairs)


def shards(
    modes, stiffness, mass_ref, areas, eigenvalues, send_list, connect, block_var, mode_weight
):
    region = lax.axis_index("region")
    mode_dev, node_count = modes.shape[1:]
    elem_count = connect.shape[1]
    flat = modes.reshape(6 * mode_dev, node_count)
    odd = region % 2
    upper = (region // 2) % 2
    order = jnp.stack([odd, 1 - odd, 2 + upper, 3 - upper]).astype(jnp.int32)
    *sent, rows = send_rows(flat, send_list, order)
    received = [swap(sent[0], "region", 0), swap(sent[1], "region", 1),
                swap_two(sent[2], "region", 0), swap_two(sent[3], "region", 1)]
    step = block_var // VAR_DEV - region
    place = jnp.where(step == 0, 0, jnp.where(step == 1 - 2 * odd, 1, 2))
    column = block_var % VAR_DEV + VAR_DEV * place
    factors = jnp.concatenate([
        jnp.broadcast_to(eigenvalues[:, None], (mode_dev, 128)), -areas.reshape(elem_count // 128, 128),
        column.reshape(1, elem_count // 32).astype(f32)], axis=0)
    own, sent_a, sent_b = main_call(
        rows, received, order, stiffness, mass_ref.transpose(0, 1, 3, 2).astype(f32), factors,
        jnp.minimum(connect, node_count + 4 * SLOTS - 1))
    sens = own + swap(sent_a, "region", 0) + swap(sent_b, "region", 1)
    weighted = jnp.sum(mode_weight[:, None] * sens, axis=0)
    other = [lax.ppermute(weighted, "mode", [(q, q ^ by) for q in range(4)]) for by in (1, 2, 3)]
    weighted = (weighted + other[0]) + (other[1] + other[2])
    return (sens, weighted)


def solution(mesh):
    in_specs = (
        P(None, "mode", "region"),
        P(None, None, None, None, "region"),
        P(),
        P("region"),
        P("mode"),
        P(None, "region"),
        P(None, "region"),
        P("region"),
        P("mode"),
    )
    out_specs = (P("mode", "region"), P("region"))
    return jax.shard_map(shards, mesh=mesh, in_specs=in_specs, out_specs=out_specs, check_vma=False)
```
